32 devices in a mesh: dp: 16 (over z, y, core), tensor: 2 (over x).
Axes of the slice: x: 2, y: 2, z: 4, core: 2. Of those that a mesh axis runs over, the one named last changes fastest.
Arguments:
- block_in: bfloat16 [16384, 1024], P(('dp', 'tensor')), may hold values from -6 to 6
- segment_ids: int32 [16, 1024], P('dp'), may hold values from 0 to 3, never falling along the last dimension, each value on 1 to 512 neighbouring positions
- cotangent: bfloat16 [16384, 1024], P(('dp', 'tensor')), may hold values from -6 to 6
- attn_gain: bfloat16 [1024], P('tensor'), may hold values from 0.5 to 1.5
- attn_shift: bfloat16 [1024], P('tensor'), may hold values from -3 to 3
- mlp_gain: bfloat16 [1024], P('tensor'), may hold values from 0.5 to 1.5
- mlp_shift: bfloat16 [1024], P('tensor'), may hold values from -3 to 3
- qkv_weight: bfloat16 [3, 1024, 1024], P(None, 'dp', 'tensor'), may hold values from -0.1875 to 0.1875
- out_weight: bfloat16 [1024, 1024], P('tensor', 'dp'), may hold values from -1 to 1
- up_weight: bfloat16 [1024, 4096], P('dp', 'tensor'), may hold values from -0.1875 to 0.1875
- up_bias: bfloat16 [4096], P('tensor'), may hold values from -3 to 3
- down_weight: bfloat16 [4096, 1024], P('tensor', 'dp'), may hold values from -0.09375 to 0.09375
- out_bias: bfloat16 [1024], P('tensor'), may hold values from -3 to 3
Outputs:
- block_out: bfloat16 [16384, 1024], P(('dp', 'tensor'))
- grad_in: float32 [16384, 1024], P(('dp', 'tensor'))
- grad_attn_gain: float32 [1024], P('tensor')
- grad_attn_shift: float32 [1024], P('tensor')
- grad_mlp_gain: float32 [1024], P('tensor')
- grad_mlp_shift: float32 [1024], P('tensor')
- grad_qkv_weight: float32 [3, 1024, 1024], P(None, 'dp', 'tensor')
- grad_out_weight: float32 [1024, 1024], P('tensor', 'dp')
- grad_up_weight: float32 [1024, 4096], P('dp', 'tensor')
- grad_up_bias: float32 [4096], P('tensor')
- grad_down_weight: float32 [4096, 1024], P('tensor', 'dp')
- grad_out_bias: float32 [1024], P('tensor')
The draws below stay inside these ranges and needn't reach their ends.
Inputs may be any that keep to these rules, and one draw needn't show every extreme that they name: `segment_ids`: document numbers never fall along a row; each document has at most half of 1024 tokens.
All inputs are finite; a program needn't handle non-finite values.
Results may differ from the reference program's by a relative error of at most 0.014.
Values may be sent and summed in bfloat16 or wider, within the bound.
A program may use at most 192 MiB of HBM per device.

```python
import math
import jax
import jax.numpy as jnp
import numpy as np
from jax import lax

D = 1024
HEADS = 16
HD = 64
ROT = 16
FF = 4096
LENGTH = 1024
SEQ_DP = 1
SEQS = 16
TOKENS = 16384
N_DP = 16


def shard_levels(own_key, extent, cuts, least, largest):
    level = 1.0
    for axis_at, shards_of in cuts:
        heights = jax.random.uniform(jax.random.fold_in(jax.random.fold_in(own_key, 6), axis_at), (shards_of,), jnp.float32, least / len(cuts), largest / len(cuts))
        level = level * jnp.repeat(jnp.exp(heights), extent[axis_at] // shards_of).reshape((-1,) + (1,) * (len(extent) - 1 - axis_at))
    return level


def length_profile(count, total, reach, skew):
    loads = [(1 << 20) // math.isqrt(standing ** skew) + 1 for standing in range(2, count + 1)]
    rest, given = total - reach - (count - 1), [1] * (count - 1)
    while rest > 0:
        movable = [i for i in range(count - 1) if given[i] < reach]
        mass, left = sum([loads[i] for i in movable]), rest
        for i in movable:
            addition = min(reach - given[i], max(1, left * loads[i] // mass), rest)
            given[i] = given[i] + addition
            rest = rest - addition
    return np.array([reach] + given)


def ragged_sizes(rng, count, total, bound, slope):
    if count == 2:
        one = jax.random.randint(rng, (), max(1, total - bound), min(bound, total - 1) + 1)
        return jnp.stack([one, total - one])
    lengths = jnp.asarray(length_profile(count, total, bound, slope), jnp.int32)
    couples = (count - 1) // 2
    donor, sink = lengths[1:1 + 2 * couples:2], lengths[2:2 + 2 * couples:2]
    room = jnp.minimum(donor - 1, bound - sink)
    passed = jax.random.randint(jax.random.fold_in(rng, 1), (couples,), 0, 1 << 20) % (room + 1)
    lengths = lengths.at[1:1 + 2 * couples:2].set(donor - passed).at[2:2 + 2 * couples:2].set(sink + passed)
    return lengths[jax.random.permutation(jax.random.fold_in(rng, 2), count)]


def gaussian(rng, shape, deviation, most, cuts=(), kind=jnp.bfloat16):
    entries = jax.random.normal(rng, shape, jnp.float32) * deviation
    if len(cuts) > 0:
        entries = shard_levels(rng, shape, cuts, -0.22, 0.18) * entries
    return jnp.clip(entries, min=-most, max=most).astype(kind)


def setup_inputs(seed: int = 0) -> dict:
    key_list = jax.random.split(jax.random.key(seed), 14)
    block_in = gaussian(key_list[0], (TOKENS, D), 1.0, 6.0, ((0, 32),))
    segment_ids = jax.vmap(lambda own: jnp.searchsorted(jnp.cumsum(ragged_sizes(own, 4, LENGTH, LENGTH // 2, 0)), jnp.arange(LENGTH), side="right"))(jax.random.split(key_list[1], SEQS)).reshape((SEQS, LENGTH)).astype(jnp.int32)
    cotangent = gaussian(key_list[2], (TOKENS, D), 1.0, 6.0, ((0, 32),))
    attn_gain = jnp.clip(1.0 + 0.1 * jax.random.normal(key_list[3], (D,), jnp.float32), 0.5, 1.5).astype(jnp.bfloat16)
    attn_shift = gaussian(key_list[4], (D,), 0.3, 3.0, ((0, 2),))
    mlp_gain = jnp.clip(1.0 + 0.1 * jax.random.normal(key_list[5], (D,), jnp.float32), 0.5, 1.5).astype(jnp.bfloat16)
    mlp_shift = gaussian(key_list[6], (D,), 0.3, 3.0, ((0, 2),))
    qkv_weight = gaussian(key_list[7], (3, D, D), D ** -0.5, 0.1875, ((1, 16), (2, 2)))
    out_weight = gaussian(key_list[8], (D, D), (D // 32) ** -0.5, 1.0, ((0, 2), (1, 16)))
    up_weight = gaussian(key_list[9], (D, FF), D ** -0.5, 0.1875, ((0, 16), (1, 2)))
    up_bias = gaussian(key_list[10], (FF,), 0.5, 3.0, ((0, 2),))
    down_weight = gaussian(key_list[11], (FF, D), FF ** -0.5, 0.09375, ((0, 2), (1, 16)))
    out_bias = gaussian(key_list[12], (D,), 0.5, 3.0, ((0, 2),))
    return {"block_in": block_in, "segment_ids": segment_ids, "cotangent": cotangent, "attn_gain": attn_gain, "attn_shift": attn_shift, "mlp_gain": mlp_gain, "mlp_shift": mlp_shift, "qkv_weight": qkv_weight, "out_weight": out_weight, "up_weight": up_weight, "up_bias": up_bias, "down_weight": down_weight, "out_bias": out_bias}


@jax.custom_vjp
def low(v):
    return lax.optimization_barrier(v.astype(jnp.bfloat16)).astype(jnp.float32)

@jax.custom_vjp
def low_back(v):
    return v

def low_keep(v):
    return (low(v), None)

def low_pass(kept, grad):
    return (grad,)

def back_keep(v):
    return (v, None)

def back_low(kept, grad):
    return (low(grad),)
low.defvjp(low_keep, low_pass)
low_back.defvjp(back_keep, back_low)
EPS = 1e-05
MASKED = -1e+30
PRECISE = lax.Precision.HIGHEST

def rope_tables(segment_rows):
    seq_count, length = segment_rows.shape
    col_index = lax.broadcasted_iota(jnp.int32, (seq_count, length), 1)
    starts_doc = jnp.concatenate([jnp.ones((seq_count, 1), jnp.bool_), segment_rows[:, 1:] != segment_rows[:, :-1]], axis=1)
    doc_start = lax.cummax(jnp.where(starts_doc, col_index, 0), axis=1)
    doc_pos = (col_index - doc_start).reshape(seq_count * length).astype(jnp.float32)
    half_rot = ROT // 2
    freq_tab = 10000.0 ** (-(jnp.arange(half_rot, dtype=jnp.float32) * 2.0) / ROT)
    angles = doc_pos[:, None] * freq_tab[None, :]
    cos_tab = jnp.concatenate([jnp.cos(angles), jnp.cos(angles)], axis=1)
    sine_tab = jnp.concatenate([jnp.sin(angles), jnp.sin(angles)], axis=1)
    return (cos_tab, sine_tab)

def rotate_fwd(row_vals, cos_tab, sine_tab):
    half_rot = ROT // 2
    head_part = row_vals[..., :ROT]
    turned = jnp.concatenate([-head_part[..., half_rot:], head_part[..., :half_rot]], axis=-1)
    return jnp.concatenate([head_part * cos_tab + turned * sine_tab, row_vals[..., ROT:]], axis=-1)

def norm_rows(row_vals, gain, shift):
    mean_row = lax.optimization_barrier(jnp.mean(row_vals, axis=-1, keepdims=True))
    centred = row_vals - mean_row
    var_row = lax.optimization_barrier(jnp.mean(centred * centred, axis=-1, keepdims=True))
    return centred * lax.rsqrt(var_row + EPS) * gain + shift

def attend_seq(pieces):
    queries, key_rows, values, seg_row = pieces
    length = seg_row.shape[0]
    scores = jnp.einsum('qhd,khd->hqk', queries, key_rows, precision=PRECISE) * (1.0 / math.sqrt(HD))
    scores = low_back(scores)
    row_pos = lax.broadcasted_iota(jnp.int32, (length, length), 0)
    col_pos = lax.broadcasted_iota(jnp.int32, (length, length), 1)
    allowed = (col_pos <= row_pos) & (seg_row[:, None] == seg_row[None, :])
    scores = jnp.where(allowed[None], scores, MASKED)
    attn_probs = jax.nn.softmax(scores, axis=-1)
    return jnp.einsum('hqk,khd->qhd', low(attn_probs), values, precision=PRECISE)

def forward(params, row_block, segment_rows):
    gain_one, shift_one, gain_two, shift_two, w_attn, w_proj, w_up, bias_up, w_down, bias_out = params
    seq_count, length = segment_rows.shape
    flat_rows = row_block.reshape(seq_count * length, D)
    h_attn = low(norm_rows(flat_rows, gain_one, shift_one))
    h_mlp = low(norm_rows(flat_rows, gain_two, shift_two))
    projected = low_back(jnp.einsum('td,cde->cte', h_attn, w_attn, precision=PRECISE))
    shaped = projected.reshape(3, seq_count * length, HEADS, HD)
    cos_tab, sine_tab = rope_tables(segment_rows)
    cos_tab = cos_tab[:, None, :]
    sine_tab = sine_tab[:, None, :]
    queries = low(rotate_fwd(shaped[0], cos_tab, sine_tab))
    key_rows = low(rotate_fwd(shaped[1], cos_tab, sine_tab))
    values = low(shaped[2])
    per_seq = (seq_count, length, HEADS, HD)
    mixture = lax.map(jax.checkpoint(attend_seq), (queries.reshape(per_seq), key_rows.reshape(per_seq), values.reshape(per_seq), segment_rows))
    attended = low_back(low(mixture.reshape(seq_count * length, D)))
    hidden_pre = low_back(jnp.dot(h_mlp, w_up, precision=PRECISE) + bias_up)
    activated = low(jax.nn.gelu(hidden_pre, approximate=False))
    return flat_rows + jnp.dot(attended, w_proj, precision=PRECISE) + jnp.dot(activated, w_down, precision=PRECISE) + bias_out

def reference(block_in, segment_ids, cotangent, attn_gain, attn_shift, mlp_gain, mlp_shift, qkv_weight, out_weight, up_weight, up_bias, down_weight, out_bias):
    params = tuple((param.astype(jnp.float32) for param in (attn_gain, attn_shift, mlp_gain, mlp_shift, qkv_weight, out_weight, up_weight, up_bias, down_weight, out_bias)))
    rows_split = block_in.astype(jnp.float32).reshape(N_DP, SEQ_DP, LENGTH, D)
    cot_split = cotangent.astype(jnp.float32).reshape(N_DP, SEQ_DP * LENGTH, D)
    seg_split = segment_ids.reshape(N_DP, SEQ_DP, LENGTH)

    def scan_step(running, pieces):
        row_block, segment_rows, grad_out = pieces

        def apply_block(param_set, inputs):
            return forward(param_set, inputs, segment_rows)
        block_result, pull_back = jax.vjp(apply_block, params, row_block)
        grad_params, grad_rows = pull_back(grad_out)
        running = jax.tree.map(lambda left, right: left + right, running, grad_params)
        return (running, (block_result.astype(jnp.bfloat16), grad_rows.reshape(SEQ_DP * LENGTH, D)))
    zero_grads = jax.tree.map(jnp.zeros_like, params)
    totals, (out_rows, grad_rows) = lax.scan(scan_step, zero_grads, (rows_split, seg_split, cot_split))
    return (out_rows.reshape(TOKENS, D), grad_rows.reshape(TOKENS, D), totals[0], totals[1], totals[2], totals[3], totals[4], totals[5], totals[6], totals[7], totals[8], totals[9])
```

```python
import functools
import math

import jax
import jax.numpy as jnp
from jax import lax
from jax.experimental import pallas as pl
from jax.experimental.pallas import tpu as pltpu
from jax.sharding import PartitionSpec as P

HD = 64
ROT = 16
PAIR = 128
Q_BLOCK = 256
SUBS = 2
EPS = 1e-05
MASKED = -1e30
MESH = pl.DeviceIdType.MESH
BF = jnp.bfloat16
F32 = jnp.float32


def nt_dot(a, b):
    return lax.dot_general(a, b, (((1,), (1,)), ((), ())), preferred_element_type=F32)


def nn_dot(a, b):
    return lax.dot_general(a, b, (((1,), (0,)), ((), ())), preferred_element_type=F32)


def tn_dot(a, b):
    return lax.dot_general(a, b, (((0,), (0,)), ((), ())), preferred_element_type=F32)


def spot_of(chip, n):
    odd, level = chip % 2, chip // 2
    return (1 - odd) * level + odd * (n - 1 - level)


def chip_of(spot, n):
    back = spot // (n // 2)
    return (1 - back) * (2 * spot) + back * (2 * (n - 1 - spot) + 1)


def places(n_dp, n_t):
    n = n_dp // 2
    dp, ten = lax.axis_index("dp"), lax.axis_index("tensor")
    core = dp % 2
    spot = spot_of(dp // 2, n)
    right = chip_of((spot + 1) % n, n) * 2 + core
    left = chip_of((spot + n - 1) % n, n) * 2 + core
    other = dp + 1 - 2 * core
    peers = [(ten + o) % n_t for o in range(1, n_t)]
    return n, dp, ten, core, spot, right, left, other, peers


def greet(ten, dp, right, left, other, peers):
    barrier = pltpu.get_barrier_semaphore()
    for to in (right, left, other):
        pl.semaphore_signal(barrier, inc=1, device_id=(to, ten), device_id_type=MESH)
    for peer in peers:
        pl.semaphore_signal(barrier, inc=1, device_id=(dp, peer), device_id_type=MESH)
    pl.semaphore_wait(barrier, 3 + len(peers))


def gather_kernel(
    n_dp, n_t, w_ref, x_ref, c_ref, p_ref, w_out, x_out, c_out, p_out,
    own_sem, t_send, t_recv, r_send, r_recv, p_send, p_recv,
):
    n, dp, ten, core, spot, right, left, other, peers = places(n_dp, n_t)
    rows, width = w_ref.shape
    piece = width // (2 * SUBS)
    greet(ten, dp, right, left, other, peers)

    def rows_at(chip):
        return pl.ds(pl.multiple_of((chip * 2 + core) * rows, rows), rows)

    pending = []
    mine = rows_at(dp // 2)
    for k, to in ((0, right), (1, left)):
        for sub in range(SUBS):
            chain = k * SUBS + sub
            cols = pl.ds(chain * piece, piece)
            copy = pltpu.make_async_remote_copy(
                src_ref=w_ref.at[:, cols], dst_ref=w_out.at[mine, cols],
                send_sem=r_send.at[chain, 0], recv_sem=r_recv.at[chain, 0],
                device_id=(to, ten), device_id_type=MESH,
            )
            copy.start()
            pending.append((copy, chain, 0))
    tcopies = []
    for o, peer in enumerate(peers):
        for a, (src, dst) in enumerate(((x_ref, x_out), (c_ref, c_out), (p_ref, p_out))):
            have = src.shape[0]
            copy = pltpu.make_async_remote_copy(
                src_ref=src,
                dst_ref=dst.at[pl.ds(pl.multiple_of(ten * have, have), have)],
                send_sem=t_send.at[o, a], recv_sem=t_recv.at[o, a],
                device_id=(dp, peer), device_id_type=MESH,
            )
            copy.start()
            tcopies.append(copy)
    pairs = []
    for chain in range(2 * SUBS):
        cols = pl.ds(chain * piece, piece)
        copy = pltpu.make_async_remote_copy(
            src_ref=w_ref.at[:, cols], dst_ref=w_out.at[mine, cols],
            send_sem=p_send.at[chain, 0], recv_sem=p_recv.at[chain, 0],
            device_id=(other, ten), device_id_type=MESH,
        )
        copy.start()
        pairs.append(copy)
    locals_ = [pltpu.make_async_copy(w_ref, w_out.at[mine], own_sem.at[0])]
    for a, (src, dst) in enumerate(((x_ref, x_out), (c_ref, c_out), (p_ref, p_out))):
        have = src.shape[0]
        locals_.append(
            pltpu.make_async_copy(
                src, dst.at[pl.ds(pl.multiple_of(ten * have, have), have)], own_sem.at[a + 1]
            )
        )
    for copy in locals_:
        copy.start()

    sends = list(copy for copy, _, _ in pending)
    held = {chain: copy for copy, chain, _ in pending}
    for step in range(1, n):
        for sub in range(SUBS):
            for k, to in ((0, right), (1, left)):
                chain = k * SUBS + sub
                cols = pl.ds(chain * piece, piece)
                held[chain].wait_recv()
                origin = (spot + n - step) % n if k == 0 else (spot + step) % n
                block = rows_at(chip_of(origin, n))
                if step < n - 1:
                    copy = pltpu.make_async_remote_copy(
                        src_ref=w_out.at[block, cols], dst_ref=w_out.at[block, cols],
                        send_sem=r_send.at[chain, step], recv_sem=r_recv.at[chain, step],
                        device_id=(to, ten), device_id_type=MESH,
                    )
                    copy.start()
                    held[chain] = copy
                    sends.append(copy)
                copy = pltpu.make_async_remote_copy(
                    src_ref=w_out.at[block, cols], dst_ref=w_out.at[block, cols],
                    send_sem=p_send.at[chain, step], recv_sem=p_recv.at[chain, step],
                    device_id=(other, ten), device_id_type=MESH,
                )
                copy.start()
                pairs.append(copy)
    for copy in sends:
        copy.wait_send()
    for copy in pairs:
        copy.wait()
    for copy in tcopies:
        copy.wait()
    for copy in locals_:
        copy.wait()


def gather_all(w_shard, x, cot, params, n_dp, n_t):
    n = n_dp // 2
    chains = 2 * SUBS
    any_spec = pl.BlockSpec(memory_space=pl.ANY)
    dma = pltpu.SemaphoreType.DMA
    return pl.pallas_call(
        functools.partial(gather_kernel, n_dp, n_t),
        out_shape=[
            jax.ShapeDtypeStruct((w_shard.shape[0] * n_dp, w_shard.shape[1]), BF),
            jax.ShapeDtypeStruct((x.shape[0] * n_t, x.shape[1]), BF),
            jax.ShapeDtypeStruct((x.shape[0] * n_t, x.shape[1]), BF),
            jax.ShapeDtypeStruct((params.shape[0] * n_t, params.shape[1]), BF),
        ],
        in_specs=[any_spec] * 4,
        out_specs=[any_spec] * 4,
        scratch_shapes=[
            dma((4,)), dma((n_t - 1, 3)), dma((n_t - 1, 3)),
            dma((chains, n - 1)), dma((chains, n - 1)), dma((chains, n)), dma((chains, n)),
        ],
        compiler_params=pltpu.CompilerParams(collective_id=0, has_side_effects=True),
        name="gather_all",
    )(w_shard, x, cot, params)


def scatter_kernel(
    n_dp, n_t, g_ref, o_ref, e_ref, g_out, o_out, e_out,
    mine, paired, landed, own_sem, t_send, t_recv, r_send, r_recv, p_send, p_recv,
):
    n, dp, ten, core, spot, right, left, other, peers = places(n_dp, n_t)
    rows, width = g_out.shape
    half = width // 2
    piece = half // SUBS
    greet(ten, dp, right, left, other, peers)

    def goal(k, step):
        return chip_of((spot + 2 * n - 1 - step) % n if k == 0 else (spot + 1 + step) % n, n)

    def rows_at(chip, whose):
        return pl.ds(pl.multiple_of((chip * 2 + whose) * rows, rows), rows)

    pairs, locals_ = {}, {}
    for step in range(n):
        for k in (0, 1):
            cols = pl.ds(k * half, half)
            pairs[k, step] = pltpu.make_async_remote_copy(
                src_ref=g_ref.at[rows_at(goal(k, step), 1 - core), cols],
                dst_ref=paired.at[k, step],
                send_sem=p_send.at[k, step], recv_sem=p_recv.at[k, step],
                device_id=(other, ten), device_id_type=MESH,
            )
            pairs[k, step].start()
            locals_[k, step] = pltpu.make_async_copy(
                g_ref.at[rows_at(goal(k, step), core), cols], mine.at[k, step],
                own_sem.at[k, step],
            )
            locals_[k, step].start()
    tcopies = []
    for o, peer in enumerate(peers):
        for a, (src, dst) in enumerate(((o_ref, o_out), (e_ref, e_out))):
            have = dst.shape[1]
            copy = pltpu.make_async_remote_copy(
                src_ref=src.at[pl.ds(pl.multiple_of(peer * have, have), have)],
                dst_ref=dst.at[o],
                send_sem=t_send.at[o, a], recv_sem=t_recv.at[o, a],
                device_id=(dp, peer), device_id_type=MESH,
            )
            copy.start()
            tcopies.append(copy)
    held, sends = {}, []
    for step in range(n):
        for sub in range(SUBS):
            cols = pl.ds(sub * piece, piece)
            for k, to in ((0, right), (1, left)):
                chain = k * SUBS + sub
                if sub == 0:
                    locals_[k, step].wait()
                    pairs[k, step].wait_recv()
                total = mine[k, step, :, cols].astype(F32) + paired[k, step, :, cols].astype(F32)
                if step > 0:
                    held[chain].wait_recv()
                    total = total + landed[chain, step - 1].astype(F32)
                if step == n - 1:
                    g_out[:, pl.ds(chain * piece, piece)] = total
                else:
                    mine[k, step, :, cols] = total.astype(BF)
                    copy = pltpu.make_async_remote_copy(
                        src_ref=mine.at[k, step, :, cols], dst_ref=landed.at[chain, step],
                        send_sem=r_send.at[chain, step], recv_sem=r_recv.at[chain, step],
                        device_id=(to, ten), device_id_type=MESH,
                    )
                    copy.start()
                    held[chain] = copy
                    sends.append(copy)
    for copy in sends:
        copy.wait_send()
    for copy in pairs.values():
        copy.wait_send()
    for copy in tcopies:
        copy.wait()


def scatter_all(grads, out_part, e_part, n_dp, n_t):
    n = n_dp // 2
    chains = 2 * SUBS
    rows, width = grads.shape[0] // n_dp, grads.shape[1]
    own = out_part.shape[0] // n_t
    any_spec = pl.BlockSpec(memory_space=pl.ANY)
    dma = pltpu.SemaphoreType.DMA
    parts = jax.ShapeDtypeStruct((n_t - 1, own, out_part.shape[1]), BF)
    return pl.pallas_call(
        functools.partial(scatter_kernel, n_dp, n_t),
        out_shape=[jax.ShapeDtypeStruct((rows, width), F32), parts, parts],
        in_specs=[any_spec] * 3,
        out_specs=[pl.BlockSpec(memory_space=pltpu.VMEM), any_spec, any_spec],
        scratch_shapes=[
            pltpu.VMEM((2, n, rows, width // 2), BF),
            pltpu.VMEM((2, n, rows, width // 2), BF),
            pltpu.VMEM((chains, n - 1, rows, width // chains), BF),
            dma((2, n)), dma((n_t - 1, 2)), dma((n_t - 1, 2)),
            dma((chains, n - 1)), dma((chains, n - 1)), dma((2, n)), dma((2, n)),
        ],
        compiler_params=pltpu.CompilerParams(
            collective_id=1, has_side_effects=True, vmem_limit_bytes=40 * 2**20
        ),
        name="scatter_all",
    )(grads, out_part, e_part)


def attend_kernel(
    q_ref, k_ref, v_ref, g_ref, cos_ref, lo_ref, hi_ref, segq_ref, segk_ref,
    att_ref, dproj_ref, dk_acc, dv_acc, dq_acc, q_s, k_s, v_s,
):
    j = pl.program_id(1)
    length = q_ref.shape[0]
    width = dproj_ref.shape[1] // 3
    back = ROT // 2
    cos, lo, hi = cos_ref[...], lo_ref[...], hi_ref[...]

    def turn(w, sign):
        up = pltpu.roll(w, PAIR - back, 1)
        down = pltpu.roll(w, back, 1)
        return w * cos + sign * (up * lo + down * hi)

    q_s[...] = (turn(q_ref[...], 1.0).astype(BF).astype(F32) * (1.0 / math.sqrt(HD))).astype(BF)
    k_s[...] = turn(k_ref[...], 1.0).astype(BF)
    v_s[...] = v_ref[...].astype(BF)
    dk_acc[...] = jnp.zeros_like(dk_acc)
    dv_acc[...] = jnp.zeros_like(dv_acc)
    first = lax.broadcasted_iota(jnp.int32, (Q_BLOCK, PAIR), 1) < HD
    reach = -(-(length // 2 - 1) // Q_BLOCK) * Q_BLOCK
    for start in range(0, length, Q_BLOCK):
        lo_key = max(0, start - reach)
        span = start + Q_BLOCK - lo_key
        keys = slice(lo_key, lo_key + span)
        rows = slice(start, start + Q_BLOCK)
        q_pos = start + lax.broadcasted_iota(jnp.int32, (Q_BLOCK, span), 0)
        k_pos = lo_key + lax.broadcasted_iota(jnp.int32, (Q_BLOCK, span), 1)
        allowed = (k_pos <= q_pos) & (segq_ref[rows, :] == segk_ref[0, :, keys])
        bias = jnp.where(allowed, 0.0, MASKED)
        q_blk, g_blk = q_s[rows, :], g_ref[rows, :]
        k_blk, v_blk = k_s[keys, :], v_s[keys, :]
        outs, dqs = [], []
        for head in (0, 1):
            pick = first if head == 0 else jnp.logical_not(first)
            q_one = jnp.where(pick, q_blk, jnp.zeros_like(q_blk))
            g_one = jnp.where(pick, g_blk, jnp.zeros_like(g_blk))
            scores = nt_dot(q_one, k_blk) + bias
            terms = jnp.exp(scores - jnp.max(scores, axis=-1, keepdims=True))
            probs = terms * (1.0 / jnp.sum(terms, axis=-1, keepdims=True))
            low = probs.astype(BF)
            outs.append(nn_dot(low, v_blk))
            weighed = nt_dot(g_one, v_blk)
            mean = jnp.sum(probs * weighed, axis=-1, keepdims=True)
            dscore = (probs * (weighed - mean)).astype(BF)
            dqs.append(nn_dot(dscore, k_blk))
            dk_acc[keys, :] += tn_dot(dscore, q_one)
            dv_acc[keys, :] += tn_dot(low, g_one)
        att_ref[rows, :] = jnp.where(first, outs[0], outs[1]).astype(BF)
        dq_acc[rows, :] = jnp.where(first, dqs[0], dqs[1])
    at = pl.multiple_of(j * PAIR, PAIR)
    dproj_ref[:, pl.ds(at, PAIR)] = turn(dq_acc[...] * (1.0 / math.sqrt(HD)), -1.0).astype(BF)
    dproj_ref[:, pl.ds(width + at, PAIR)] = turn(dk_acc[...], -1.0).astype(BF)
    dproj_ref[:, pl.ds(2 * width + at, PAIR)] = dv_acc[...].astype(BF)


def attend(projected, grad_mix, tables, segment_ids):
    seqs, length = segment_ids.shape
    tokens, width = grad_mix.shape
    pairs = width // PAIR
    seg_col = segment_ids.reshape(tokens, 1)
    seg_row = segment_ids.reshape(seqs, 1, length)

    def col(at):
        return pl.BlockSpec((length, PAIR), lambda s, j: (s, j + at * pairs))

    table = pl.BlockSpec((length, PAIR), lambda s, j: (s, 0))
    return pl.pallas_call(
        attend_kernel,
        grid=(seqs, pairs),
        out_shape=[
            jax.ShapeDtypeStruct((tokens, width), BF),
            jax.ShapeDtypeStruct((tokens, 3 * width), BF),
        ],
        in_specs=[
            col(0), col(1), col(2), col(0), table, table, table,
            pl.BlockSpec((length, 1), lambda s, j: (s, 0)),
            pl.BlockSpec((1, 1, length), lambda s, j: (s, 0, 0)),
        ],
        out_specs=[col(0), pl.BlockSpec((length, 3 * width), lambda s, j: (s, 0))],
        scratch_shapes=[pltpu.VMEM((length, PAIR), F32)] * 3
        + [pltpu.VMEM((length, PAIR), BF)] * 3,
        compiler_params=pltpu.CompilerParams(vmem_limit_bytes=48 * 2**20),
        name="attend",
    )(projected, projected, projected, grad_mix, *tables, seg_col, seg_row)


def hidden_kernel(h_ref, c_ref, up_ref, down_ref, b_ref, act_ref, pre_ref, sum_ref):
    hidden = nn_dot(h_ref[...], up_ref[...]) + b_ref[...]
    pulled = nn_dot(c_ref[...], down_ref[...])
    phi = 0.5 + 0.5 * lax.erf(hidden * math.sqrt(0.5))
    act_ref[...] = (hidden * phi).astype(BF)
    density = jnp.exp(-0.5 * hidden * hidden) * (1.0 / math.sqrt(2.0 * math.pi))
    pre = (pulled * (phi + hidden * density)).astype(BF)
    pre_ref[...] = pre
    sum_ref[...] = jnp.sum(pre.astype(F32), axis=0, keepdims=True)


def hidden_branch(h_mlp, cot, weights, up_at, down_at, up_bias):
    tokens, model = h_mlp.shape
    ff = up_bias.shape[1]
    tile, chunk = 256, 1024
    return pl.pallas_call(
        hidden_kernel,
        grid=(tokens // chunk, ff // tile),
        out_shape=[
            jax.ShapeDtypeStruct((tokens, ff), BF),
            jax.ShapeDtypeStruct((tokens, ff), BF),
            jax.ShapeDtypeStruct((tokens // chunk, 1, ff), F32),
        ],
        in_specs=[
            pl.BlockSpec((chunk, model), lambda s, j: (s, 0)),
            pl.BlockSpec((chunk, model), lambda s, j: (s, 0)),
            pl.BlockSpec((model, tile), lambda s, j: (0, up_at // tile + j)),
            pl.BlockSpec((model, tile), lambda s, j: (0, down_at // tile + j)),
            pl.BlockSpec((1, tile), lambda s, j: (0, j)),
        ],
        out_specs=[
            pl.BlockSpec((chunk, tile), lambda s, j: (s, j)),
            pl.BlockSpec((chunk, tile), lambda s, j: (s, j)),
            pl.BlockSpec((None, 1, tile), lambda s, j: (s, 0, j)),
        ],
        compiler_params=pltpu.CompilerParams(vmem_limit_bytes=48 * 2**20),
        name="hidden_branch",
    )(h_mlp, cot, weights, weights, up_bias)


def rope_tables(segment_rows):
    seqs, length = segment_rows.shape
    col_index = lax.broadcasted_iota(jnp.int32, (seqs, length), 1)
    starts_doc = jnp.concatenate(
        [jnp.ones((seqs, 1), jnp.bool_), segment_rows[:, 1:] != segment_rows[:, :-1]], axis=1
    )
    doc_start = lax.cummax(jnp.where(starts_doc, col_index, 0), axis=1)
    doc_pos = (col_index - doc_start).reshape(seqs * length).astype(F32)
    half = ROT // 2
    freq = 10000.0 ** (-(jnp.arange(half, dtype=F32) * 2.0) / ROT)
    angles = doc_pos[:, None] * freq[None, :]
    cos, sine = jnp.cos(angles), jnp.sin(angles)
    zero = jnp.zeros_like(cos)
    one_rest = jnp.ones((seqs * length, HD - ROT), F32)
    zero_rest = jnp.zeros((seqs * length, HD - ROT), F32)
    reps = (1, PAIR // HD)
    return (
        jnp.tile(jnp.concatenate([cos, cos, one_rest], axis=1), reps),
        jnp.tile(jnp.concatenate([-sine, zero, zero_rest], axis=1), reps),
        jnp.tile(jnp.concatenate([zero, sine, zero_rest], axis=1), reps),
    )


def per_device(
    n_dp, n_t, block_in, segment_ids, cotangent, attn_gain, attn_shift, mlp_gain, mlp_shift,
    qkv_weight, out_weight, up_weight, up_bias, down_weight, out_bias,
):
    ten = lax.axis_index("tensor")
    wide, ff = out_weight.shape[0], up_weight.shape[1]
    own_rows, model = block_in.shape
    share = model // n_t
    w_shard = jnp.concatenate(
        [qkv_weight[0], qkv_weight[1], qkv_weight[2], out_weight.T, up_weight, down_weight.T],
        axis=1,
    )
    vectors = jnp.stack([attn_gain, attn_shift, mlp_gain, mlp_shift, out_bias])
    vectors = jnp.pad(vectors, ((0, 11), (0, 0)))
    w_all, rows_in, cot_rows, vec_all = gather_all(
        w_shard, block_in, cotangent, vectors, n_dp, n_t
    )
    vec_all = vec_all.reshape(n_t, 16, share).transpose(1, 0, 2).reshape(16, model).astype(F32)
    gain_one, shift_one, gain_two, shift_two, bias_out = (vec_all[i] for i in range(5))
    at_out, at_up, at_down = 3 * wide, 4 * wide, 4 * wide + ff
    w_qkv, w_out = w_all[:, :at_out], w_all[:, at_out:at_up]
    w_up, w_down = w_all[:, at_up:at_down], w_all[:, at_down:]
    tables = rope_tables(segment_ids)

    vals = rows_in.astype(F32)
    mean_row = jnp.mean(vals, axis=-1, keepdims=True)
    centred = vals - mean_row
    inv_dev = lax.rsqrt(jnp.mean(centred * centred, axis=-1, keepdims=True) + EPS)
    normed = centred * inv_dev
    h_attn = (normed * gain_one + shift_one).astype(BF)
    h_mlp = (normed * gain_two + shift_two).astype(BF)

    projected = nn_dot(h_attn, w_qkv)
    grad_mix = nn_dot(cot_rows, w_out).astype(BF)
    attended, grad_proj = attend(projected, grad_mix, tables, segment_ids)
    act, grad_pre, up_sums = hidden_branch(
        h_mlp, cot_rows, w_all, at_up, at_down, up_bias.astype(F32).reshape(1, ff)
    )
    partial_out = (nt_dot(attended, w_out) + nt_dot(act, w_down)).astype(BF)

    grad_one = nt_dot(grad_proj, w_qkv)
    grad_two = nt_dot(grad_pre, w_up)
    e_part = (grad_one * gain_one + grad_two * gain_two).astype(BF)
    own_cot = cotangent.astype(F32)
    placed = lax.dynamic_update_slice(
        jnp.zeros((n_t * ff,), F32), jnp.sum(up_sums, axis=(0, 1)), (ten * ff,)
    )
    small = jnp.concatenate([
        jnp.sum(grad_one * normed, axis=0), jnp.sum(grad_one, axis=0),
        jnp.sum(grad_two * normed, axis=0), jnp.sum(grad_two, axis=0),
        jnp.sum(own_cot, axis=0), placed,
    ])
    small = lax.psum(small, ("dp", "tensor"))

    grads = jnp.concatenate(
        [
            tn_dot(h_attn, grad_proj).astype(BF), tn_dot(cot_rows, attended).astype(BF),
            tn_dot(h_mlp, grad_pre).astype(BF), tn_dot(cot_rows, act).astype(BF),
        ],
        axis=1,
    )
    shard, out_got, e_got = scatter_all(grads, partial_out, e_part, n_dp, n_t)

    start = ten * own_rows
    def own(array):
        return lax.dynamic_slice_in_dim(array, start, own_rows, 0)

    summed = own(partial_out).astype(F32) + jnp.sum(out_got.astype(F32), axis=0)
    out_rows = (block_in.astype(F32) + bias_out + summed).astype(BF)
    e_sum = own(e_part).astype(F32) + jnp.sum(e_got.astype(F32), axis=0)
    own_normed, own_inv = own(normed), own(inv_dev)
    grad_rows = own_cot + own_inv * (
        e_sum
        - jnp.mean(e_sum, axis=-1, keepdims=True)
        - own_normed * jnp.mean(e_sum * own_normed, axis=-1, keepdims=True)
    )

    def part(index):
        return lax.dynamic_slice_in_dim(small, index * model + ten * share, share, 0)

    up_grad_bias = lax.dynamic_slice_in_dim(small, 5 * model + ten * ff, ff, 0)
    shard_qkv = jnp.stack([shard[:, c * wide : (c + 1) * wide] for c in range(3)])
    return (
        out_rows, grad_rows, part(0), part(1), part(2), part(3),
        shard_qkv, shard[:, at_out:at_up].T, shard[:, at_up:at_down],
        up_grad_bias, shard[:, at_down:].T, part(4),
    )


def solution(mesh):
    n_dp, n_t = mesh.shape["dp"], mesh.shape["tensor"]
    both = P(("dp", "tensor"), None)
    vec = P("tensor")
    return jax.shard_map(
        functools.partial(per_device, n_dp, n_t),
        mesh=mesh,
        in_specs=(
            both, P("dp", None), both, vec, vec, vec, vec,
            P(None, "dp", "tensor"), P("tensor", "dp"), P("dp", "tensor"), vec,
            P("tensor", "dp"), vec,
        ),
        out_specs=(
            both, both, vec, vec, vec, vec,
            P(None, "dp", "tensor"), P("tensor", "dp"), P("dp", "tensor"), vec,
            P("tensor", "dp"), vec,
        ),
        check_vma=False,
    )
```
